32 devices in a mesh: req: 8 (over y, x, core), kv: 4 (over z).
Axes of the slice: x: 2, y: 2, z: 4, core: 2. Of those that a mesh axis runs over, the one named last changes fastest.
Arguments:
- hidden: bfloat16 [512, 2048], P('req', 'kv'), may hold values from -6 to 6
- attn_gain: float32 [2048], replicated, may hold values from 0.25 to 1.75
- q_gain: float32 [128], replicated, may hold values from 0.25 to 1.75
- k_gain: float32 [128], replicated, may hold values from 0.25 to 1.75
- w_q: bfloat16 [2048, 2048], P(None, 'kv'), may hold values from -0.125 to 0.125
- w_gate_attn: bfloat16 [2048, 2048], P(None, 'kv'), may hold values from -0.125 to 0.125
- w_k: bfloat16 [2048, 1024], P(None, 'kv'), may hold values from -0.125 to 0.125
- w_v: bfloat16 [2048, 1024], P(None, 'kv'), may hold values from -0.125 to 0.125
- w_o: bfloat16 [2048, 2048], P('kv'), may hold values from -0.125 to 0.125
- k_pool: bfloat16 [1200, 128, 1024], P('req', None, 'kv'), may hold values from -245 to 245
- v_pool: bfloat16 [1200, 128, 1024], P('req', None, 'kv'), may hold values from -6 to 6
- lengths: int32 [512], P('req'), may hold values from 1 to 4095, as said below
- page_table: int32 [512, 32], P('req'), may hold values from 0 to 149, as said below
- mig_request: int32 [8, 8], P('req'), may hold values from 0 to 63, as said below
- mig_dest: int32 [8, 8], P('req'), may hold values from 0 to 7, as said below
- mlp_gain: float32 [2048], replicated, may hold values from 0.25 to 1.75
- w_gate: bfloat16 [2048, 6144], P(None, ('req', 'kv')), may hold values from -0.125 to 0.125
- w_up: bfloat16 [2048, 6144], P(None, ('req', 'kv')), may hold values from -0.125 to 0.125
- w_down: bfloat16 [2048, 6144], P(None, ('req', 'kv')), may hold values from -0.078125 to 0.078125
Outputs:
- out_hidden: bfloat16 [512, 2048], P('req', 'kv')
- mig_keys: bfloat16 [64, 512, 1024], P('req', None, 'kv')
- mig_values: bfloat16 [64, 512, 1024], P('req', None, 'kv')
The draws below stay inside these ranges and needn't reach their ends.
Inputs may be any that keep to these rules, and one draw needn't show every extreme that they name: lengths[r] tokens of request r are cached and its new token takes position lengths[r]; some request holds 4095 cached tokens. `page_table`: entries refer to the pool of the request's own device. The first lengths[r] // 128 + 1 entries of row r are the request's pages, distinct and never shared with another request of that device; later entries are valid pages that are not read. `mig_request`: row s names 8 different requests of device s; each has at most 511 cached tokens, and in every row one has exactly that many. `mig_dest`: each row is a permutation.
All inputs are finite; a program needn't handle non-finite values.
Results may differ from the reference program's by a relative error of at most 0.0093.
Values may be sent and summed in bfloat16 or wider, within the bound.
A program may use at most 128 MiB of HBM per device.

```python
import jax
import jax.numpy as jnp
from jax import lax

D = 2048
H = 16
KVH = 8
HD = 128
FF = 6144
R_DEV = 64
PAGE = 128
MAXP = 32
MIGP = 4
REQS = 512
POOL_DEV = 150
N_REQ = 8


def permute_rows(key, row_number, length):
    split_keys = jax.random.split(key, row_number)

    def one_row(row_key):
        return jax.random.permutation(row_key, length)
    return jax.vmap(one_row)(split_keys)


def layout(key):
    heavy_total = max(1, N_REQ // 8)
    dev_order = jax.random.permutation(jax.random.fold_in(key, 11), N_REQ)
    heavy_dev = (dev_order < heavy_total)[:, None]
    local_rank = permute_rows(jax.random.fold_in(key, 12), N_REQ, R_DEV)
    migrant = local_rank < N_REQ
    long_one = heavy_dev & (local_rank >= N_REQ) & (local_rank < N_REQ + 2)
    mid_pages = jax.random.randint(jax.random.fold_in(key, 13), (N_REQ, R_DEV), 2, MIGP + 1)
    page_count = jnp.where(migrant, jnp.where(local_rank == 0, MIGP, mid_pages), jnp.where(long_one, MAXP, 1))
    spread = jax.random.randint(jax.random.fold_in(key, 14), (N_REQ, R_DEV), 1, PAGE)
    length_rows = (page_count - 1) * PAGE + spread
    at_most = (local_rank == 0) | long_one & (local_rank == N_REQ)
    length_rows = jnp.where(at_most, page_count * PAGE - 1, length_rows)
    offsets = jnp.cumsum(page_count, axis=1) - page_count
    shuffle = permute_rows(jax.random.fold_in(key, 15), N_REQ, POOL_DEV)
    slot_ids = jnp.arange(MAXP, dtype=jnp.int32)
    table_pos = offsets[:, :, None] + jnp.minimum(slot_ids[None, None, :], page_count[:, :, None] - 1)
    page_rows = jnp.take_along_axis(shuffle, table_pos.reshape(N_REQ, R_DEV * MAXP), axis=1)
    page_rows = page_rows.reshape(N_REQ * R_DEV, MAXP)
    mig_rows = jnp.argsort(local_rank, axis=1)[:, :N_REQ]
    return (length_rows.reshape(N_REQ * R_DEV).astype(jnp.int32), page_rows.astype(jnp.int32), mig_rows.astype(jnp.int32))


def draw_lengths(key, part):
    return layout(key)[0]


def draw_page_table(key, part):
    return layout(key)[1]


def draw_mig_request(key, part):
    return layout(key)[2]


def draw_mig_dest(key, part):
    return permute_rows(jax.random.fold_in(key, 16), N_REQ, N_REQ).astype(jnp.int32)


def draw_k_pool(key, part):
    full_shape = (N_REQ * POOL_DEV, PAGE, KVH * HD)
    base_draw = jnp.clip(jax.random.normal(jax.random.fold_in(key, 21), full_shape, jnp.float32), -3.0, 3.0)
    return base_draw.astype(jnp.bfloat16)


def block_levels(stream_key, dims, cuts, low, largest):
    gain = 1.0
    for dim, parts in cuts:
        draws = jax.random.uniform(jax.random.fold_in(jax.random.fold_in(stream_key, 6), dim), (parts,), jnp.float32, low / len(cuts), largest / len(cuts))
        gain = gain * jnp.repeat(jnp.exp(draws), dims[dim] // parts).reshape((-1,) + (1,) * (len(dims) - 1 - dim))
    return gain


def bell_draw(stream_key, dims, deviation, most, cuts=(), kind=jnp.bfloat16):
    entries = deviation * jax.random.normal(stream_key, dims, jnp.float32)
    if cuts:
        entries = entries * block_levels(stream_key, dims, cuts, -0.22, 0.18)
    return jnp.clip(entries, -most, most).astype(kind)


def setup_inputs(seed: int = 0) -> dict:
    key_of = jax.random.split(jax.random.key(seed), 20)
    return {
        "hidden": bell_draw(key_of[0], (REQS, D), 1.0, 6.0, ((0, 8), (1, 4))),
        "attn_gain": jnp.clip(1.0 + 0.15 * jax.random.normal(key_of[1], (D,), jnp.float32), 0.25, 1.75),
        "q_gain": jnp.clip(1.0 + 0.15 * jax.random.normal(key_of[2], (HD,), jnp.float32), 0.25, 1.75),
        "k_gain": jnp.clip(1.0 + 0.15 * jax.random.normal(key_of[3], (HD,), jnp.float32), 0.25, 1.75),
        "w_q": bell_draw(key_of[4], (D, H * HD), D ** -0.5, 0.125, ((1, 4),)),
        "w_gate_attn": bell_draw(key_of[5], (D, H * HD), D ** -0.5, 0.125, ((1, 4),)),
        "w_k": bell_draw(key_of[6], (D, KVH * HD), D ** -0.5, 0.125, ((1, 4),)),
        "w_v": bell_draw(key_of[7], (D, KVH * HD), D ** -0.5, 0.125, ((1, 4),)),
        "w_o": bell_draw(key_of[8], (H * HD, D), (H * HD) ** -0.5, 0.125, ((0, 4),)),
        "k_pool": draw_k_pool(jax.random.fold_in(key_of[19], 71), 0),
        "v_pool": bell_draw(key_of[10], (N_REQ * POOL_DEV, PAGE, KVH * HD), 1.0, 6.0, ((0, 8), (2, 4))),
        "lengths": draw_lengths(jax.random.fold_in(key_of[19], 71), 0),
        "page_table": draw_page_table(jax.random.fold_in(key_of[19], 71), 0),
        "mig_request": draw_mig_request(jax.random.fold_in(key_of[19], 71), 0),
        "mig_dest": draw_mig_dest(jax.random.fold_in(key_of[19], 71), 0),
        "mlp_gain": jnp.clip(1.0 + 0.15 * jax.random.normal(key_of[15], (D,), jnp.float32), 0.25, 1.75),
        "w_gate": bell_draw(key_of[16], (D, FF), D ** -0.5, 0.125, ((1, 32),)),
        "w_up": bell_draw(key_of[17], (D, FF), D ** -0.5, 0.125, ((1, 32),)),
        "w_down": bell_draw(key_of[18], (D, FF), FF ** -0.5, 0.078125, ((1, 32),)),
    }


EPSILON = 1e-06
ROPE_BASE = 1000000.0

def rms_norm(values, scale_row):
    values = values.astype(jnp.float32)
    return values * lax.rsqrt(lax.optimization_barrier(jnp.mean(values * values, axis=-1, keepdims=True)) + EPSILON) * scale_row

def rotate(values, position):
    half_dim = values.shape[-1] // 2
    frequency = ROPE_BASE ** (-jnp.arange(half_dim, dtype=jnp.float32) * 2.0 / values.shape[-1])
    angles = position.astype(jnp.float32)[:, None, None] * frequency
    cosine = jnp.cos(angles)
    sine_part = jnp.sin(angles)
    first_half = values[..., :half_dim]
    second = values[..., half_dim:]
    return jnp.concatenate([first_half * cosine - second * sine_part, second * cosine + first_half * sine_part], axis=-1)

def reference(hidden, attn_gain, q_gain, k_gain, w_q, w_gate_attn, w_k, w_v, w_o, k_pool, v_pool, lengths, page_table, mig_request, mig_dest, mlp_gain, w_gate, w_up, w_down):
    group_size = H // KVH
    slot_span = MAXP * PAGE
    score_scale = HD ** (-0.5)
    normed = rms_norm(hidden, attn_gain).astype(jnp.bfloat16)
    query_raw = jnp.dot(normed, w_q, preferred_element_type=jnp.float32).reshape(REQS, H, HD)
    gate_raw = jnp.dot(normed, w_gate_attn, preferred_element_type=jnp.float32)
    key_raw = jnp.dot(normed, w_k, preferred_element_type=jnp.float32).reshape(REQS, KVH, HD)
    value_raw = jnp.dot(normed, w_v, preferred_element_type=jnp.float32).reshape(REQS, KVH, HD)
    queries = rotate(rms_norm(query_raw, q_gain), lengths).astype(jnp.bfloat16)
    new_keys = rotate(rms_norm(key_raw, k_gain), lengths).astype(jnp.bfloat16)
    new_values = value_raw.astype(jnp.bfloat16)
    owners = jnp.arange(REQS, dtype=jnp.int32) // R_DEV
    pool_pages = page_table + (owners * POOL_DEV)[:, None]
    position = jnp.arange(slot_span, dtype=jnp.int32)

    def attend(request_items):
        one_query, key_new, value_new, page_ids, length = request_items
        cached_keys = k_pool[page_ids].reshape(slot_span, KVH, HD).astype(jnp.float32)
        cached_values = v_pool[page_ids].reshape(slot_span, KVH, HD).astype(jnp.float32)
        grouped = one_query.astype(jnp.float32).reshape(KVH, group_size, HD)
        scores = jnp.einsum('kgd,tkd->kgt', grouped, cached_keys) * score_scale
        scores = jnp.where(position < length, scores, -jnp.inf)
        own_score = jnp.einsum('kgd,kd->kg', grouped, key_new.astype(jnp.float32)) * score_scale
        row_top = jnp.maximum(lax.optimization_barrier(jnp.max(scores, axis=-1)), own_score)
        exps_all = jnp.exp(scores - row_top[..., None])
        own_exp = jnp.exp(own_score - row_top)
        denom_sum = lax.optimization_barrier(jnp.sum(exps_all, axis=-1)) + own_exp
        weights = lax.optimization_barrier((exps_all / denom_sum[..., None]).astype(jnp.bfloat16)).astype(jnp.float32)
        own_weight = lax.optimization_barrier((own_exp / denom_sum).astype(jnp.bfloat16)).astype(jnp.float32)
        context = jnp.einsum('kgt,tkd->kgd', weights, cached_values)
        context = context + own_weight[..., None] * value_new.astype(jnp.float32)[:, None, :]
        return context.reshape(H * HD)
    context = lax.map(attend, (queries, new_keys, new_values, pool_pages, lengths))
    gated = (jax.nn.sigmoid(gate_raw) * context).astype(jnp.bfloat16)
    mid_stream = (hidden.astype(jnp.float32) + jnp.dot(gated, w_o, preferred_element_type=jnp.float32)).astype(jnp.bfloat16)
    normed_mlp = rms_norm(mid_stream, mlp_gain).astype(jnp.bfloat16)
    gate_part = jnp.dot(normed_mlp, w_gate, preferred_element_type=jnp.float32)
    up_part = jnp.dot(normed_mlp, w_up, preferred_element_type=jnp.float32)
    activation = (jax.nn.silu(gate_part) * up_part).astype(jnp.bfloat16)
    down_part = jnp.dot(activation, w_down.T, preferred_element_type=jnp.float32)
    out_hidden = (mid_stream.astype(jnp.float32) + down_part).astype(jnp.bfloat16)
    src_flat = jnp.repeat(jnp.arange(N_REQ, dtype=jnp.int32), N_REQ)
    moved_rows = src_flat * R_DEV + mig_request.reshape(-1).astype(jnp.int32)
    moved_pages = page_table[moved_rows, :MIGP] + (src_flat * POOL_DEV)[:, None]
    slot_count = MIGP * PAGE
    slot_pos = jnp.arange(slot_count, dtype=jnp.int32)[None, :, None]
    moved_len = lengths[moved_rows][:, None, None]
    zero_value = jnp.zeros((), jnp.bfloat16)
    target = mig_dest.reshape(-1).astype(jnp.int32) * N_REQ + src_flat

    def place_cache(pool, fresh_rows):
        cached = pool[moved_pages].reshape(N_REQ * N_REQ, slot_count, KVH * HD)
        fresh_row = fresh_rows.reshape(REQS, KVH * HD)[moved_rows][:, None, :]
        filled = jnp.where(slot_pos < moved_len, cached, jnp.where(slot_pos == moved_len, fresh_row, zero_value))
        return jnp.zeros((N_REQ * N_REQ, slot_count, KVH * HD), jnp.bfloat16).at[target].set(filled)
    mig_keys = place_cache(k_pool, new_keys)
    mig_values = place_cache(v_pool, new_values)
    return (out_hidden, mig_keys, mig_values)
```

```python
import functools

import jax
import jax.numpy as jnp
from jax import lax
from jax.experimental import pallas as pl
from jax.experimental.pallas import tpu as pltpu
from jax.sharding import PartitionSpec as P

MIGP = 4
EPSILON = 1e-06
ROPE_BASE = 1000000.0
ROWS = 8
LOW = -1e30


def rms_norm(values, scale_row):
    values = values.astype(jnp.float32)
    return (
        values * lax.rsqrt(jnp.mean(values * values, axis=-1, keepdims=True) + EPSILON) * scale_row
    )


def rotate(values, position):
    half_dim = values.shape[-1] // 2
    frequency = ROPE_BASE ** (-jnp.arange(half_dim, dtype=jnp.float32) * 2.0 / values.shape[-1])
    angles = position.astype(jnp.float32)[:, None, None] * frequency
    cosine = jnp.cos(angles)
    sine_part = jnp.sin(angles)
    first_half = values[..., :half_dim]
    second = values[..., half_dim:]
    return jnp.concatenate(
        [first_half * cosine - second * sine_part, second * cosine + first_half * sine_part],
        axis=-1,
    )


def page_owners(page_table, lengths, pool_pages, page_size):
    req_count, slots = page_table.shape
    slot = jnp.arange(slots, dtype=jnp.int32)[None, :]
    used = slot <= (lengths // page_size)[:, None]
    table = jnp.where(used, page_table, -1).reshape(1, -1)
    code = jnp.arange(req_count * slots, dtype=jnp.int32)[None, :]
    hit = table == jnp.arange(pool_pages, dtype=jnp.int32)[:, None]
    return jnp.max(jnp.where(hit, code, -1), axis=1)


def attend_kernel(
    slots, group, blocks, per_block, page_size, scale,
    code_ref, len_ref, q_ref, k_new_ref, v_new_ref, k_ref, v_ref,
    out_ref, scores, top, total, acc,
):
    step = pl.program_id(0)
    head_dim = out_ref.shape[-1]
    kv_local = k_ref.shape[-1] // head_dim
    lane = lax.broadcasted_iota(jnp.int32, (ROWS, page_size), 1)
    row = lax.broadcasted_iota(jnp.int32, (ROWS, head_dim), 0)

    def own_scores():
        folded = q_ref[:, :, :head_dim]
        for k in range(1, kv_local):
            folded = folded + q_ref[:, :, k * head_dim : (k + 1) * head_dim]
        return jnp.sum(folded * k_new_ref[...], axis=-1, keepdims=True) * scale

    @pl.when(step == 0)
    def _():
        top[...] = jnp.broadcast_to(own_scores(), top.shape)

    @pl.when(step < blocks)
    def _():
        for j in range(per_block):
            page = step * per_block + j
            code = code_ref[page]
            owner = jnp.maximum(code, 0) // slots
            left = jnp.where(code < 0, 0, len_ref[owner] - lax.rem(code, slots) * page_size)
            s = lax.dot_general(
                q_ref[owner].astype(jnp.bfloat16),
                k_ref[j],
                (((1,), (1,)), ((), ())),
                preferred_element_type=jnp.float32,
            )
            s = jnp.where(lane < left, s * scale, LOW)
            scores[page] = s
            top[owner] = jnp.maximum(top[owner], s)

    @pl.when(step == blocks)
    def _():
        peak = jnp.max(top[...], axis=-1, keepdims=True)
        top[...] = jnp.broadcast_to(peak, top.shape)
        own = jnp.exp(own_scores() - peak)
        wide_lane = lax.broadcasted_iota(jnp.int32, total.shape, 2)
        total[...] = jnp.where(wide_lane == 0, own, 0.0)
        acc[...] = own * v_new_ref[...]

    @pl.when(step >= blocks)
    def _():
        for j in range(per_block):
            page = (step - blocks) * per_block + j
            owner = jnp.maximum(code_ref[page], 0) // slots
            e = jnp.exp(scores[page] - top[owner])
            total[owner] = total[owner] + e
            o = jnp.dot(e.astype(jnp.bfloat16), v_ref[j], preferred_element_type=jnp.float32)
            picked = o[:, :head_dim]
            for k in range(1, kv_local):
                picked = jnp.where(
                    row // group == k, o[:, k * head_dim : (k + 1) * head_dim], picked
                )
            acc[owner] = acc[owner] + picked

    @pl.when(step == 2 * blocks - 1)
    def _():
        out_ref[...] = acc[...] / jnp.sum(total[...], axis=-1, keepdims=True)


def attend(queries, new_keys, new_values, k_pool, v_pool, lengths, page_table):
    req_count, kv_local, group, head_dim = queries.shape
    pool_pages, page_size, channels = k_pool.shape
    slots = page_table.shape[1]
    heads = kv_local * group
    per_block = max(b for b in range(1, 17) if pool_pages % b == 0)
    blocks = pool_pages // per_block
    code = page_owners(page_table, lengths, pool_pages, page_size)
    which = jnp.eye(kv_local, dtype=jnp.float32)[None, :, None, :, None]
    spread = (queries.astype(jnp.float32)[:, :, :, None, :] * which).reshape(
        req_count, heads, channels
    )
    pad = ((0, 0), (0, ROWS - heads), (0, 0))
    spread = jnp.pad(spread, pad)

    def by_head(values):
        values = jnp.repeat(values.astype(jnp.float32), group, axis=1)
        return jnp.pad(values, pad)

    whole = pl.BlockSpec((req_count, ROWS, channels), lambda i, *_: (0, 0, 0))
    slim = pl.BlockSpec((req_count, ROWS, head_dim), lambda i, *_: (0, 0, 0))
    out = pl.pallas_call(
        functools.partial(
            attend_kernel, slots, group, blocks, per_block, page_size, head_dim ** (-0.5)
        ),
        out_shape=jax.ShapeDtypeStruct((req_count, ROWS, head_dim), jnp.float32),
        grid_spec=pltpu.PrefetchScalarGridSpec(
            num_scalar_prefetch=2,
            grid=(2 * blocks,),
            in_specs=[
                whole,
                slim,
                slim,
                pl.BlockSpec(
                    (per_block, page_size, channels),
                    lambda i, *_: (jnp.minimum(i, blocks - 1), 0, 0),
                ),
                pl.BlockSpec(
                    (per_block, page_size, channels),
                    lambda i, *_: (jnp.maximum(i - blocks, 0), 0, 0),
                ),
            ],
            out_specs=slim,
            scratch_shapes=[
                pltpu.VMEM((pool_pages, ROWS, page_size), jnp.float32),
                pltpu.VMEM((req_count, ROWS, page_size), jnp.float32),
                pltpu.VMEM((req_count, ROWS, page_size), jnp.float32),
                pltpu.VMEM((req_count, ROWS, head_dim), jnp.float32),
            ],
        ),
        compiler_params=pltpu.CompilerParams(
            dimension_semantics=("arbitrary",), vmem_limit_bytes=32 * 1024 * 1024
        ),
        cost_estimate=pl.CostEstimate(
            flops=4 * pool_pages * page_size * channels * ROWS,
            bytes_accessed=2 * pool_pages * page_size * channels * 2,
            transcendentals=pool_pages * page_size * ROWS,
        ),
        name="attend_pool",
    )(code, lengths, spread, by_head(new_keys), by_head(new_values), k_pool, v_pool)
    return out[:, :heads]


def pack_kernel(page_ref, len_ref, *refs):
    pages = MIGP
    out_ref = refs[2 * pages]
    page_size = refs[0].shape[1]
    row = lax.broadcasted_iota(jnp.int32, refs[0].shape[1:], 0)
    for side in range(2):
        for t in range(pages):
            block = refs[side * pages + t][0]
            keep = row + t * page_size < len_ref[0]
            out_ref[side, t * page_size : (t + 1) * page_size] = jnp.where(
                keep, block, jnp.zeros_like(block)
            )


def pack_block(pages, length, k_pool, v_pool):
    _, page_size, channels = k_pool.shape
    span = MIGP * page_size

    def page_spec(t):
        return pl.BlockSpec((1, page_size, channels), lambda i, page_ref, len_ref: (page_ref[t], 0, 0))

    return pl.pallas_call(
        pack_kernel,
        out_shape=jax.ShapeDtypeStruct((2, span, channels), jnp.bfloat16),
        grid_spec=pltpu.PrefetchScalarGridSpec(
            num_scalar_prefetch=2,
            grid=(1,),
            in_specs=[page_spec(t) for _ in range(2) for t in range(MIGP)],
            out_specs=pl.BlockSpec((2, span, channels), lambda i, *_: (0, 0, 0)),
        ),
        cost_estimate=pl.CostEstimate(
            flops=0, bytes_accessed=8 * span * channels, transcendentals=0
        ),
        name="pack_block",
    )(pages, length, *([k_pool] * MIGP), *([v_pool] * MIGP))


def place_kernel(count, where_ref, len_ref, fresh_ref, *refs):
    blocks, k_out, v_out = refs[:count], refs[count], refs[count + 1]
    span, channels = blocks[0].shape[1:]
    row = lax.broadcasted_iota(jnp.int32, (span, channels), 0)
    for s in range(count):
        slot = where_ref[s]
        for side, out in enumerate((k_out, v_out)):
            new = fresh_ref[s, :, side * channels : (side + 1) * channels]
            out[slot] = jnp.where(row == len_ref[s], new, blocks[s][side])


def place_blocks(where, lengths, fresh, blocks):
    count = len(blocks)
    _, span, channels = blocks[0].shape
    shape = jax.ShapeDtypeStruct((count, span, channels), jnp.bfloat16)
    smem = pl.BlockSpec(memory_space=pltpu.SMEM)
    vmem = pl.BlockSpec(memory_space=pltpu.VMEM)
    return pl.pallas_call(
        functools.partial(place_kernel, count),
        out_shape=(shape, shape),
        in_specs=[smem, smem, vmem] + [vmem] * count,
        out_specs=(vmem, vmem),
        compiler_params=pltpu.CompilerParams(vmem_limit_bytes=40 * 1024 * 1024),
        name="place_blocks",
    )(where, lengths, fresh, *blocks)


def per_device(
    hidden,
    attn_gain,
    q_gain,
    k_gain,
    w_q,
    w_gate_attn,
    w_k,
    w_v,
    w_o,
    k_pool,
    v_pool,
    lengths,
    page_table,
    mig_request,
    mig_dest,
    mlp_gain,
    w_gate,
    w_up,
    w_down,
):
    head_dim = q_gain.shape[0]
    req_count = hidden.shape[0]
    kv_local = w_k.shape[1] // head_dim
    q_local = w_q.shape[1] // head_dim
    group_size = q_local // kv_local
    channels = kv_local * head_dim
    model_width = mlp_gain.shape[0]
    req_groups = lax.axis_size("req")
    me = lax.axis_index("req")

    mig_rows = mig_request[0]
    dest_row = mig_dest[0]
    partner = me ^ jnp.arange(req_groups, dtype=jnp.int32)
    chosen = dest_row[None, :] == partner[:, None]
    send_rows = jnp.sum(jnp.where(chosen, mig_rows[None, :], 0), axis=1)
    send_len = lengths[send_rows]
    send_pages = page_table[send_rows, :MIGP]
    packed = [
        pack_block(send_pages[s], send_len[s : s + 1], k_pool, v_pool) for s in range(req_groups)
    ]
    arrived = [packed[0]] + [
        lax.ppermute(packed[s], "req", [(i, i ^ s) for i in range(req_groups)])
        for s in range(1, req_groups)
    ]

    whole_rows = lax.all_gather(hidden, "kv", axis=1, tiled=True)
    normed = rms_norm(whole_rows, attn_gain).astype(jnp.bfloat16)
    query_raw = jnp.dot(normed, w_q, preferred_element_type=jnp.float32).reshape(
        req_count, q_local, head_dim
    )
    gate_raw = jnp.dot(normed, w_gate_attn, preferred_element_type=jnp.float32)
    key_raw = jnp.dot(normed, w_k, preferred_element_type=jnp.float32).reshape(
        req_count, kv_local, head_dim
    )
    value_raw = jnp.dot(normed, w_v, preferred_element_type=jnp.float32).reshape(
        req_count, kv_local, head_dim
    )
    queries = rotate(rms_norm(query_raw, q_gain), lengths).astype(jnp.bfloat16)
    queries = queries.reshape(req_count, kv_local, group_size, head_dim)
    new_keys = rotate(rms_norm(key_raw, k_gain), lengths).astype(jnp.bfloat16)
    new_values = value_raw.astype(jnp.bfloat16)

    fresh = jnp.concatenate(
        [new_keys.reshape(req_count, channels), new_values.reshape(req_count, channels)], axis=1
    )
    by_dest = jnp.sum(
        jnp.where(
            dest_row[None, :] == jnp.arange(req_groups, dtype=jnp.int32)[:, None],
            mig_rows[None, :],
            0,
        ),
        axis=1,
    )
    dest_len = lengths[by_dest]
    digits = jnp.stack([dest_len // 256, dest_len % 256], axis=1).astype(jnp.bfloat16)
    notes = jnp.concatenate([fresh[by_dest], jnp.pad(digits, ((0, 0), (0, 126)))], axis=1)
    all_notes = lax.all_gather(notes, "req", axis=0, tiled=False)
    mine = lax.dynamic_index_in_dim(all_notes, me, 1, keepdims=False)[partner]
    width = 2 * channels
    got_digits = mine[:, width : width + 2].astype(jnp.int32)
    got_len = got_digits[:, 0] * 256 + got_digits[:, 1]
    mig_keys, mig_values = place_blocks(partner, got_len, mine[:, None, :width], arrived)

    context = attend(queries, new_keys, new_values, k_pool, v_pool, lengths, page_table)
    gated = (jax.nn.sigmoid(gate_raw) * context.reshape(req_count, q_local * head_dim)).astype(
        jnp.bfloat16
    )
    head_terms = jnp.dot(gated, w_o, preferred_element_type=jnp.float32)
    attn_sum = lax.psum(head_terms, "kv")
    mid_stream = (whole_rows.astype(jnp.float32) + attn_sum).astype(jnp.bfloat16)
    normed_mlp = rms_norm(mid_stream, mlp_gain).astype(jnp.bfloat16)
    kv_count = lax.axis_size("kv")
    slice_width = model_width // kv_count
    slice_start = lax.axis_index("kv") * slice_width
    mid_slice = lax.dynamic_slice_in_dim(mid_stream, slice_start, slice_width, 1)
    row_piece = lax.all_gather(normed_mlp, "req", axis=0, tiled=True)
    gate_part = jnp.dot(row_piece, w_gate, preferred_element_type=jnp.float32)
    up_part = jnp.dot(row_piece, w_up, preferred_element_type=jnp.float32)
    activation = (jax.nn.silu(gate_part) * up_part).astype(jnp.bfloat16)
    unit_count = activation.shape[1]
    grouped_act = activation.reshape(req_groups, req_count, unit_count)
    grouped_down = w_down.reshape(kv_count, slice_width, unit_count)
    term = jnp.einsum(
        "gru,hcu->ghrc", grouped_act, grouped_down, preferred_element_type=jnp.float32
    )
    term = term.reshape(req_groups * kv_count, req_count, slice_width)
    mlp_part = lax.psum_scatter(term, ("req", "kv"), scatter_dimension=0, tiled=True)[0]
    out_hidden = (mid_slice.astype(jnp.float32) + mlp_part).astype(jnp.bfloat16)
    return (out_hidden, mig_keys, mig_values)


def solution(mesh):
    return jax.shard_map(
        per_device,
        mesh=mesh,
        in_specs=(
            P("req", "kv"),
            P(),
            P(),
            P(),
            P(None, "kv"),
            P(None, "kv"),
            P(None, "kv"),
            P(None, "kv"),
            P("kv", None),
            P("req", None, "kv"),
            P("req", None, "kv"),
            P("req"),
            P("req", None),
            P("req", None),
            P("req", None),
            P(),
            P(None, ("req", "kv")),
            P(None, ("req", "kv")),
            P(None, ("req", "kv")),
        ),
        out_specs=(P("req", "kv"), P("req", None, "kv"), P("req", None, "kv")),
        check_vma=False,
    )
```

```python
import functools

import jax
import jax.numpy as jnp
from jax import lax
from jax.experimental import pallas as pl
from jax.experimental.pallas import tpu as pltpu
from jax.sharding import PartitionSpec as P

MIGP = 4
EPSILON = 1e-06
ROPE_BASE = 1000000.0
ROWS = 8
LOW = -1e30


def rms_norm(values, scale_row):
    values = values.astype(jnp.float32)
    return (
        values * lax.rsqrt(jnp.mean(values * values, axis=-1, keepdims=True) + EPSILON) * scale_row
    )


def rotate(values, position):
    half_dim = values.shape[-1] // 2
    frequency = ROPE_BASE ** (-jnp.arange(half_dim, dtype=jnp.float32) * 2.0 / values.shape[-1])
    angles = position.astype(jnp.float32)[:, None, None] * frequency
    cosine = jnp.cos(angles)
    sine_part = jnp.sin(angles)
    first_half = values[..., :half_dim]
    second = values[..., half_dim:]
    return jnp.concatenate(
        [first_half * cosine - second * sine_part, second * cosine + first_half * sine_part],
        axis=-1,
    )


def page_owners(page_table, lengths, pool_pages, page_size):
    req_count, slots = page_table.shape
    slot = jnp.arange(slots, dtype=jnp.int32)[None, :]
    used = slot <= (lengths // page_size)[:, None]
    table = jnp.where(used, page_table, -1).reshape(1, -1)
    code = jnp.arange(req_count * slots, dtype=jnp.int32)[None, :]
    hit = table == jnp.arange(pool_pages, dtype=jnp.int32)[:, None]
    return jnp.max(jnp.where(hit, code, -1), axis=1)


def attend_kernel(
    slots, group, blocks, per_block, page_size, scale,
    code_ref, len_ref, q_ref, k_new_ref, v_new_ref, k_ref, v_ref,
    out_ref, scores, top, total, acc,
):
    step = pl.program_id(0)
    head_dim = out_ref.shape[-1]
    kv_local = k_ref.shape[-1] // head_dim
    lane = lax.broadcasted_iota(jnp.int32, (ROWS, page_size), 1)
    row = lax.broadcasted_iota(jnp.int32, (ROWS, head_dim), 0)

    def own_scores():
        folded = q_ref[:, :, :head_dim]
        for k in range(1, kv_local):
            folded = folded + q_ref[:, :, k * head_dim : (k + 1) * head_dim]
        return jnp.sum(folded * k_new_ref[...], axis=-1, keepdims=True) * scale

    @pl.when(step == 0)
    def _():
        top[...] = jnp.broadcast_to(own_scores(), top.shape)

    @pl.when(step < blocks)
    def _():
        for j in range(per_block):
            page = step * per_block + j
            code = code_ref[page]
            owner = jnp.maximum(code, 0) // slots
            left = jnp.where(code < 0, 0, len_ref[owner] - lax.rem(code, slots) * page_size)
            s = lax.dot_general(
                q_ref[owner].astype(jnp.bfloat16),
                k_ref[j],
                (((1,), (1,)), ((), ())),
                preferred_element_type=jnp.float32,
            )
            s = jnp.where(lane < left, s * scale, LOW)
            scores[page] = s
            top[owner] = jnp.maximum(top[owner], s)

    @pl.when(step == blocks)
    def _():
        peak = jnp.max(top[...], axis=-1, keepdims=True)
        top[...] = jnp.broadcast_to(peak, top.shape)
        own = jnp.exp(own_scores() - peak)
        wide_lane = lax.broadcasted_iota(jnp.int32, total.shape, 2)
        total[...] = jnp.where(wide_lane == 0, own, 0.0)
        acc[...] = own * v_new_ref[...]

    @pl.when(step >= blocks)
    def _():
        for j in range(per_block):
            page = (step - blocks) * per_block + j
            owner = jnp.maximum(code_ref[page], 0) // slots
            e = jnp.exp(scores[page] - top[owner])
            total[owner] = total[owner] + e
            o = jnp.dot(e.astype(jnp.bfloat16), v_ref[j], preferred_element_type=jnp.float32)
            picked = o[:, :head_dim]
            for k in range(1, kv_local):
                picked = jnp.where(
                    row // group == k, o[:, k * head_dim : (k + 1) * head_dim], picked
                )
            acc[owner] = acc[owner] + picked

    @pl.when(step == 2 * blocks - 1)
    def _():
        out_ref[...] = acc[...] / jnp.sum(total[...], axis=-1, keepdims=True)


def attend(queries, new_keys, new_values, k_pool, v_pool, lengths, page_table):
    req_count, kv_local, group, head_dim = queries.shape
    pool_pages, page_size, channels = k_pool.shape
    slots = page_table.shape[1]
    heads = kv_local * group
    per_block = max(b for b in range(1, 17) if pool_pages % b == 0)
    blocks = pool_pages // per_block
    code = page_owners(page_table, lengths, pool_pages, page_size)
    which = jnp.eye(kv_local, dtype=jnp.float32)[None, :, None, :, None]
    spread = (queries.astype(jnp.float32)[:, :, :, None, :] * which).reshape(
        req_count, heads, channels
    )
    pad = ((0, 0), (0, ROWS - heads), (0, 0))
    spread = jnp.pad(spread, pad)

    def by_head(values):
        values = jnp.repeat(values.astype(jnp.float32), group, axis=1)
        return jnp.pad(values, pad)

    whole = pl.BlockSpec((req_count, ROWS, channels), lambda i, *_: (0, 0, 0))
    slim = pl.BlockSpec((req_count, ROWS, head_dim), lambda i, *_: (0, 0, 0))
    out = pl.pallas_call(
        functools.partial(
            attend_kernel, slots, group, blocks, per_block, page_size, head_dim ** (-0.5)
        ),
        out_shape=jax.ShapeDtypeStruct((req_count, ROWS, head_dim), jnp.float32),
        grid_spec=pltpu.PrefetchScalarGridSpec(
            num_scalar_prefetch=2,
            grid=(2 * blocks,),
            in_specs=[
                whole,
                slim,
                slim,
                pl.BlockSpec(
                    (per_block, page_size, channels),
                    lambda i, *_: (jnp.minimum(i, blocks - 1), 0, 0),
                ),
                pl.BlockSpec(
                    (per_block, page_size, channels),
                    lambda i, *_: (jnp.maximum(i - blocks, 0), 0, 0),
                ),
            ],
            out_specs=slim,
            scratch_shapes=[
                pltpu.VMEM((pool_pages, ROWS, page_size), jnp.float32),
                pltpu.VMEM((req_count, ROWS, page_size), jnp.float32),
                pltpu.VMEM((req_count, ROWS, page_size), jnp.float32),
                pltpu.VMEM((req_count, ROWS, head_dim), jnp.float32),
            ],
        ),
        compiler_params=pltpu.CompilerParams(
            dimension_semantics=("arbitrary",), vmem_limit_bytes=56 * 1024 * 1024
        ),
        cost_estimate=pl.CostEstimate(
            flops=4 * pool_pages * page_size * channels * ROWS,
            bytes_accessed=2 * pool_pages * page_size * channels * 2,
            transcendentals=pool_pages * page_size * ROWS,
        ),
        name="attend_pool",
    )(code, lengths, spread, by_head(new_keys), by_head(new_values), k_pool, v_pool)
    return out[:, :heads]


def pack_kernel(count, page_ref, len_ref, *refs):
    outs = refs[2 * MIGP :]
    step = pl.program_id(0)
    page_size = refs[0].shape[1]
    row = lax.broadcasted_iota(jnp.int32, refs[0].shape[1:], 0)
    for s in range(count):

        @pl.when(step == s)
        def _():
            for side in range(2):
                for t in range(MIGP):
                    block = refs[side * MIGP + t][0]
                    keep = row + t * page_size < len_ref[s]
                    outs[s][side, t * page_size : (t + 1) * page_size] = jnp.where(
                        keep, block, jnp.zeros_like(block)
                    )


def pack_blocks(pages, lengths, k_pool, v_pool):
    _, page_size, channels = k_pool.shape
    count = lengths.shape[0]
    span = MIGP * page_size

    def page_spec(t):
        return pl.BlockSpec(
            (1, page_size, channels), lambda i, page_ref, len_ref: (page_ref[i * MIGP + t], 0, 0)
        )

    return pl.pallas_call(
        functools.partial(pack_kernel, count),
        out_shape=[jax.ShapeDtypeStruct((2, span, channels), jnp.bfloat16)] * count,
        grid_spec=pltpu.PrefetchScalarGridSpec(
            num_scalar_prefetch=2,
            grid=(count,),
            in_specs=[page_spec(t) for _ in range(2) for t in range(MIGP)],
            out_specs=[pl.BlockSpec((2, span, channels), lambda i, *_: (0, 0, 0))] * count,
        ),
        compiler_params=pltpu.CompilerParams(vmem_limit_bytes=48 * 1024 * 1024),
        name="pack_blocks",
    )(pages.reshape(-1), lengths, *([k_pool] * MIGP), *([v_pool] * MIGP))


def place_kernel(count, where_ref, len_ref, fresh_ref, *refs):
    blocks, k_out, v_out = refs[:count], refs[count], refs[count + 1]
    span, channels = blocks[0].shape[1:]
    row = lax.broadcasted_iota(jnp.int32, (span, channels), 0)
    for s in range(count):
        slot = where_ref[s]
        for side, out in enumerate((k_out, v_out)):
            new = fresh_ref[s, :, side * channels : (side + 1) * channels]
            out[slot] = jnp.where(row == len_ref[s], new, blocks[s][side])


def place_blocks(where, lengths, fresh, blocks):
    count = len(blocks)
    _, span, channels = blocks[0].shape
    shape = jax.ShapeDtypeStruct((count, span, channels), jnp.bfloat16)
    smem = pl.BlockSpec(memory_space=pltpu.SMEM)
    vmem = pl.BlockSpec(memory_space=pltpu.VMEM)
    return pl.pallas_call(
        functools.partial(place_kernel, count),
        out_shape=(shape, shape),
        in_specs=[smem, smem, vmem] + [vmem] * count,
        out_specs=(vmem, vmem),
        compiler_params=pltpu.CompilerParams(vmem_limit_bytes=40 * 1024 * 1024),
        name="place_blocks",
    )(where, lengths, fresh, *blocks)


def greet(peers):
    barrier = pltpu.get_barrier_semaphore()
    for peer in peers:
        pl.semaphore_signal(
            barrier, inc=1, device_id=peer, device_id_type=pl.DeviceIdType.MESH
        )
    pl.semaphore_wait(barrier, len(peers))


def send(source, target, send_sem, recv_sem, peer):
    copy = pltpu.make_async_remote_copy(
        src_ref=source,
        dst_ref=target,
        send_sem=send_sem,
        recv_sem=recv_sem,
        device_id=peer,
        device_id_type=pl.DeviceIdType.MESH,
    )
    copy.start()
    return copy


def ring(axis, n):
    me = lax.axis_index(axis)
    return [{axis: lax.rem(me + d, n)} for d in range(1, n)]


def row_norm(pieces, gain_ref, out_ref):
    width = pieces.shape[2]
    n = pieces.shape[0]
    squares = 0.0
    for k in range(n):
        block = pieces[k].astype(jnp.float32)
        squares = squares + jnp.sum(block * block, axis=-1, keepdims=True)
    factor = lax.rsqrt(squares / (n * width) + EPSILON)
    for k in range(n):
        cols = slice(k * width, (k + 1) * width)
        block = pieces[k].astype(jnp.float32)
        out_ref[:, cols] = (block * factor * gain_ref[:, cols]).astype(out_ref.dtype)


def norm_kernel(n, hidden_ref, gain_ref, out_ref, pieces, send_sem, recv_sem):
    me = lax.axis_index("kv")
    peers = ring("kv", n)
    greet(peers)
    copies = [
        send(hidden_ref, pieces.at[me], send_sem.at[d], recv_sem.at[d], peer)
        for d, peer in enumerate(peers)
    ]
    pieces[me] = hidden_ref[...]
    for copy in copies:
        copy.wait()
    row_norm(pieces, gain_ref, out_ref)


def gathered_norm(hidden, gain, n):
    rows, width = hidden.shape
    return pl.pallas_call(
        functools.partial(norm_kernel, n),
        out_shape=jax.ShapeDtypeStruct((rows, n * width), jnp.bfloat16),
        in_specs=[pl.BlockSpec(memory_space=pltpu.VMEM)] * 2,
        out_specs=pl.BlockSpec(memory_space=pltpu.VMEM),
        scratch_shapes=[
            pltpu.VMEM((n, rows, width), jnp.bfloat16),
            pltpu.SemaphoreType.DMA((n - 1,)),
            pltpu.SemaphoreType.DMA((n - 1,)),
        ],
        compiler_params=pltpu.CompilerParams(collective_id=0, has_side_effects=True),
        name="gathered_norm",
    )(hidden, gain[None])


def merge_kernel(
    n, groups, gated_ref, w_ref, hidden_ref, gain_ref, notes_ref,
    mid_ref, normed_ref, got_ref,
    parts, came, mids, got, part_s, part_r, mid_s, mid_r, note_s, note_r,
):
    me = lax.axis_index("kv")
    mine = lax.axis_index("req")
    width = hidden_ref.shape[1]
    peers = ring("kv", n)
    others = ring("req", groups)
    greet(peers + others)
    copies = []
    for d, peer in enumerate(others):
        copies.append(
            send(notes_ref.at[peer["req"]], got.at[mine], note_s.at[d], note_r.at[d], peer)
        )
    got[mine] = notes_ref[mine]

    def part(k):
        cols = pl.ds(pl.multiple_of(k * width, 128), width)
        return jnp.dot(gated_ref[...], w_ref[:, cols], preferred_element_type=jnp.float32)

    part_copies = []
    for d, peer in enumerate(peers):
        parts[d] = part(peer["kv"]).astype(parts.dtype)
        part_copies.append(send(parts.at[d], came.at[d], part_s.at[d], part_r.at[d], peer))
    total = hidden_ref[...].astype(jnp.float32) + part(me)
    for d, copy in enumerate(part_copies):
        copy.wait()
        total = total + came[d].astype(jnp.float32)
    mid_ref[...] = total.astype(mid_ref.dtype)
    mids[me] = total.astype(mid_ref.dtype)
    mid_copies = [
        send(mid_ref, mids.at[me], mid_s.at[d], mid_r.at[d], peer) for d, peer in enumerate(peers)
    ]
    for copy in mid_copies:
        copy.wait()
    row_norm(mids, gain_ref, normed_ref)
    for copy in copies:
        copy.wait()
    got_ref[...] = got[...]


def merged_norm(gated, w_o, hidden, gain, notes, n, groups):
    rows, width = hidden.shape
    dma = pltpu.SemaphoreType.DMA
    vmem = pl.BlockSpec(memory_space=pltpu.VMEM)
    return pl.pallas_call(
        functools.partial(merge_kernel, n, groups),
        out_shape=(
            jax.ShapeDtypeStruct((rows, width), jnp.bfloat16),
            jax.ShapeDtypeStruct((rows, n * width), jnp.bfloat16),
            jax.ShapeDtypeStruct(notes.shape, notes.dtype),
        ),
        in_specs=[vmem] * 5,
        out_specs=(vmem,) * 3,
        scratch_shapes=[
            pltpu.VMEM((n - 1, rows, width), jnp.bfloat16),
            pltpu.VMEM((n - 1, rows, width), jnp.bfloat16),
            pltpu.VMEM((n, rows, width), jnp.bfloat16),
            pltpu.VMEM(notes.shape, notes.dtype),
            dma((n - 1,)), dma((n - 1,)), dma((n - 1,)), dma((n - 1,)),
            dma((groups - 1,)), dma((groups - 1,)),
        ],
        compiler_params=pltpu.CompilerParams(
            collective_id=1, has_side_effects=True, vmem_limit_bytes=32 * 1024 * 1024
        ),
        name="merged_norm",
    )(gated, w_o, hidden, gain[None], notes)


def mlp_kernel(
    n, groups, normed_ref, gate_ref, up_ref, down_ref, mid_ref, out_ref,
    rows, own, pair_out, pair_in, chip_out, chip_in, line_out, line_in,
    a_s, a_r, b_s, b_r, p_s, p_r, c_s, c_r, z_s, z_r,
):
    me = lax.axis_index("req")
    kv = lax.axis_index("kv")
    pairs = groups // 2
    pair, core = me // 2, lax.rem(me, 2)
    sibling = {"req": pair * 2 + 1 - core}
    peers = ring("kv", n)
    far = [{"req": lax.rem(pair + d, pairs) * 2 + core} for d in range(1, pairs)]
    greet(peers + far + [sibling])
    count, width = mid_ref.shape

    def at(d):
        return lax.rem(pair - d + pairs, pairs)

    far_copies = [
        send(normed_ref, rows.at[me], a_s.at[d], a_r.at[d], peer) for d, peer in enumerate(far)
    ]
    forwards = [send(normed_ref, rows.at[me], b_s.at[0], b_r.at[0], sibling)]
    rows[me] = normed_ref[...]
    pair_copies = []
    chip_copies = []

    def reduce(d):
        pair_copies[d].wait()
        total = own[d] + pair_in[d].astype(jnp.float32)
        if d == 0:
            own[0] = total
            return
        chip_out[d - 1] = total.astype(chip_out.dtype)
        target = {"req": at(d) * 2 + core}
        chip_copies.append(
            send(chip_out.at[d - 1], chip_in.at[d - 1], c_s.at[d - 1], c_r.at[d - 1], target)
        )

    for d in range(pairs):
        if d > 0:
            far_copies[d - 1].wait()
            held = rows.at[at(d) * 2 + core]
            forwards.append(send(held, held, b_s.at[d], b_r.at[d], sibling))
        forwards[d].wait()
        block = rows[pl.ds(at(d) * 2, 2)].reshape(2 * count, n * width)
        gate = jnp.dot(block, gate_ref[...], preferred_element_type=jnp.float32)
        up = jnp.dot(block, up_ref[...], preferred_element_type=jnp.float32)
        act = (gate / (1.0 + jnp.exp(-gate)) * up).astype(jnp.bfloat16)
        term = lax.dot_general(
            act, down_ref[...], (((1,), (1,)), ((), ())), preferred_element_type=jnp.float32
        )
        low, high = term[:count], term[count:]
        own[d] = jnp.where(core == 0, low, high)
        pair_out[d] = jnp.where(core == 0, high, low).astype(pair_out.dtype)
        pair_copies.append(
            send(pair_out.at[d], pair_in.at[d], p_s.at[d], p_r.at[d], sibling)
        )
        if d > 0:
            reduce(d - 1)
    reduce(pairs - 1)
    for d, copy in enumerate(chip_copies):
        copy.wait()
        own[0] = own[0] + chip_in[d].astype(jnp.float32)
    line_copies = []
    for d, peer in enumerate(peers):
        cols = pl.ds(pl.multiple_of(peer["kv"] * width, 128), width)
        line_out[d] = own[0, :, cols].astype(line_out.dtype)
        line_copies.append(send(line_out.at[d], line_in.at[d], z_s.at[d], z_r.at[d], peer))
    total = mid_ref[...].astype(jnp.float32)
    total = total + own[0, :, pl.ds(pl.multiple_of(kv * width, 128), width)]
    for d, copy in enumerate(line_copies):
        copy.wait()
        total = total + line_in[d].astype(jnp.float32)
    out_ref[...] = total.astype(out_ref.dtype)


def mlp(normed, w_gate, w_up, w_down, mid, n, groups):
    rows, width = mid.shape
    pairs = groups // 2
    wide = n * width
    dma = pltpu.SemaphoreType.DMA
    vmem = pl.BlockSpec(memory_space=pltpu.VMEM)
    half = jnp.bfloat16
    return pl.pallas_call(
        functools.partial(mlp_kernel, n, groups),
        out_shape=jax.ShapeDtypeStruct((rows, width), half),
        in_specs=[vmem] * 5,
        out_specs=vmem,
        scratch_shapes=[
            pltpu.VMEM((groups, rows, wide), half),
            pltpu.VMEM((pairs, rows, wide), jnp.float32),
            pltpu.VMEM((pairs, rows, wide), half),
            pltpu.VMEM((pairs, rows, wide), half),
            pltpu.VMEM((pairs - 1, rows, wide), half),
            pltpu.VMEM((pairs - 1, rows, wide), half),
            pltpu.VMEM((n - 1, rows, width), half),
            pltpu.VMEM((n - 1, rows, width), half),
            dma((pairs - 1,)), dma((pairs - 1,)),
            dma((pairs,)), dma((pairs,)),
            dma((pairs,)), dma((pairs,)),
            dma((pairs - 1,)), dma((pairs - 1,)),
            dma((n - 1,)), dma((n - 1,)),
        ],
        compiler_params=pltpu.CompilerParams(
            collective_id=2, has_side_effects=True, vmem_limit_bytes=48 * 1024 * 1024
        ),
        name="mlp_exchange",
    )(normed, w_gate, w_up, w_down, mid)


def per_device(
    hidden,
    attn_gain,
    q_gain,
    k_gain,
    w_q,
    w_gate_attn,
    w_k,
    w_v,
    w_o,
    k_pool,
    v_pool,
    lengths,
    page_table,
    mig_request,
    mig_dest,
    mlp_gain,
    w_gate,
    w_up,
    w_down,
):
    head_dim = q_gain.shape[0]
    req_count = hidden.shape[0]
    kv_local = w_k.shape[1] // head_dim
    q_local = w_q.shape[1] // head_dim
    group_size = q_local // kv_local
    channels = kv_local * head_dim
    req_groups = lax.axis_size("req")
    me = lax.axis_index("req")

    mig_rows = mig_request[0]
    dest_row = mig_dest[0]
    partner = me ^ jnp.arange(req_groups, dtype=jnp.int32)
    chosen = dest_row[None, :] == partner[:, None]
    send_rows = jnp.sum(jnp.where(chosen, mig_rows[None, :], 0), axis=1)
    send_len = lengths[send_rows]
    send_pages = page_table[send_rows, :MIGP]
    kv_count = lax.axis_size("kv")
    packed = pack_blocks(send_pages, send_len, k_pool, v_pool)
    packed, hidden = lax.optimization_barrier((packed, hidden))
    arrived = [packed[0]] + [
        lax.ppermute(packed[s], "req", [(i, i ^ s) for i in range(req_groups)])
        for s in range(1, req_groups)
    ]

    normed = gathered_norm(hidden, attn_gain, kv_count)
    query_raw = jnp.dot(normed, w_q, preferred_element_type=jnp.float32).reshape(
        req_count, q_local, head_dim
    )
    gate_raw = jnp.dot(normed, w_gate_attn, preferred_element_type=jnp.float32)
    key_raw = jnp.dot(normed, w_k, preferred_element_type=jnp.float32).reshape(
        req_count, kv_local, head_dim
    )
    value_raw = jnp.dot(normed, w_v, preferred_element_type=jnp.float32).reshape(
        req_count, kv_local, head_dim
    )
    queries = rotate(rms_norm(query_raw, q_gain), lengths).astype(jnp.bfloat16)
    queries = queries.reshape(req_count, kv_local, group_size, head_dim)
    new_keys = rotate(rms_norm(key_raw, k_gain), lengths).astype(jnp.bfloat16)
    new_values = value_raw.astype(jnp.bfloat16)

    fresh = jnp.concatenate(
        [new_keys.reshape(req_count, channels), new_values.reshape(req_count, channels)], axis=1
    )
    by_dest = jnp.sum(
        jnp.where(
            dest_row[None, :] == jnp.arange(req_groups, dtype=jnp.int32)[:, None],
            mig_rows[None, :],
            0,
        ),
        axis=1,
    )
    dest_len = lengths[by_dest].astype(jnp.float32)
    width = 2 * channels
    notes = jnp.concatenate(
        [fresh[by_dest].astype(jnp.float32), jnp.broadcast_to(dest_len[:, None], (req_groups, 128))],
        axis=1,
    )
    notes = jnp.broadcast_to(notes[:, None, :], (req_groups, 8, width + 128))
    context = attend(queries, new_keys, new_values, k_pool, v_pool, lengths, page_table)
    gated = (jax.nn.sigmoid(gate_raw) * context.reshape(req_count, q_local * head_dim)).astype(
        jnp.bfloat16
    )
    mid_slice, normed_mlp, got = merged_norm(
        gated, w_o, hidden, mlp_gain, notes, kv_count, req_groups
    )
    arrived, normed_mlp = lax.optimization_barrier((arrived, normed_mlp))
    mine = got[partner, 0]
    got_len = mine[:, width].astype(jnp.int32)
    mig_keys, mig_values = place_blocks(
        partner, got_len, mine[:, None, :width].astype(jnp.bfloat16), arrived
    )
    out_hidden = mlp(normed_mlp, w_gate, w_up, w_down, mid_slice, kv_count, req_groups)
    return (out_hidden, mig_keys, mig_values)


def solution(mesh):
    return jax.shard_map(
        per_device,
        mesh=mesh,
        in_specs=(
            P("req", "kv"),
            P(),
            P(),
            P(),
            P(None, "kv"),
            P(None, "kv"),
            P(None, "kv"),
            P(None, "kv"),
            P("kv", None),
            P("req", None, "kv"),
            P("req", None, "kv"),
            P("req"),
            P("req", None),
            P("req", None),
            P("req", None),
            P(),
            P(None, ("req", "kv")),
            P(None, ("req", "kv")),
            P(None, ("req", "kv")),
        ),
        out_specs=(P("req", "kv"), P("req", None, "kv"), P("req", None, "kv")),
        check_vma=False,
    )
```

```python
import functools

import jax
import jax.numpy as jnp
from jax import lax
from jax.experimental import pallas as pl
from jax.experimental.pallas import tpu as pltpu
from jax.sharding import PartitionSpec as P

MIGP = 4
EPSILON = 1e-06
ROPE_BASE = 1000000.0
ROWS = 8
LOW = -1e30


def rms_norm(values, scale_row):
    values = values.astype(jnp.float32)
    return (
        values * lax.rsqrt(jnp.mean(values * values, axis=-1, keepdims=True) + EPSILON) * scale_row
    )


def rotate(values, position):
    half_dim = values.shape[-1] // 2
    frequency = ROPE_BASE ** (-jnp.arange(half_dim, dtype=jnp.float32) * 2.0 / values.shape[-1])
    angles = position.astype(jnp.float32)[:, None, None] * frequency
    cosine = jnp.cos(angles)
    sine_part = jnp.sin(angles)
    first_half = values[..., :half_dim]
    second = values[..., half_dim:]
    return jnp.concatenate(
        [first_half * cosine - second * sine_part, second * cosine + first_half * sine_part],
        axis=-1,
    )


def page_owners(page_table, lengths, pool_pages, page_size):
    req_count, slots = page_table.shape
    slot = jnp.arange(slots, dtype=jnp.int32)[None, :]
    used = slot <= (lengths // page_size)[:, None]
    table = jnp.where(used, page_table, -1).reshape(1, -1)
    code = jnp.arange(req_count * slots, dtype=jnp.int32)[None, :]
    hit = table == jnp.arange(pool_pages, dtype=jnp.int32)[:, None]
    return jnp.max(jnp.where(hit, code, -1), axis=1)


def attend_kernel(
    slots, group, blocks, per_block, page_size, scale,
    code_ref, len_ref, q_ref, k_new_ref, v_new_ref, *refs,
):
    streams = (len(refs) - 5) // 2
    k_refs, v_refs = refs[:streams], refs[streams : 2 * streams]
    out_ref, scores, top, total, acc = refs[2 * streams :]
    each = per_block // streams
    step = pl.program_id(0)
    head_dim = out_ref.shape[-1]
    kv_local = k_refs[0].shape[-1] // head_dim
    lane = lax.broadcasted_iota(jnp.int32, (ROWS, page_size), 1)
    row = lax.broadcasted_iota(jnp.int32, (ROWS, head_dim), 0)

    def own_scores():
        folded = q_ref[:, :, :head_dim]
        for k in range(1, kv_local):
            folded = folded + q_ref[:, :, k * head_dim : (k + 1) * head_dim]
        return jnp.sum(folded * k_new_ref[...], axis=-1, keepdims=True) * scale

    @pl.when(step == 0)
    def _():
        top[...] = jnp.broadcast_to(own_scores(), top.shape)

    @pl.when(step < blocks)
    def _():
        for j in range(per_block):
            page = step * per_block + j
            code = code_ref[page]
            owner = jnp.maximum(code, 0) // slots
            left = jnp.where(code < 0, 0, len_ref[owner] - lax.rem(code, slots) * page_size)
            s = lax.dot_general(
                q_ref[owner].astype(jnp.bfloat16),
                k_refs[j // each][j % each],
                (((1,), (1,)), ((), ())),
                preferred_element_type=jnp.float32,
            )
            s = jnp.where(lane < left, s * scale, LOW)
            scores[page] = s
            top[owner] = jnp.maximum(top[owner], s)

    @pl.when(step == blocks)
    def _():
        peak = jnp.max(top[...], axis=-1, keepdims=True)
        top[...] = jnp.broadcast_to(peak, top.shape)
        own = jnp.exp(own_scores() - peak)
        wide_lane = lax.broadcasted_iota(jnp.int32, total.shape, 2)
        total[...] = jnp.where(wide_lane == 0, own, 0.0)
        acc[...] = own * v_new_ref[...]

    @pl.when(step >= blocks)
    def _():
        for j in range(per_block):
            page = (step - blocks) * per_block + j
            owner = jnp.maximum(code_ref[page], 0) // slots
            e = jnp.exp(scores[page] - top[owner])
            total[owner] = total[owner] + e
            o = jnp.dot(e.astype(jnp.bfloat16), v_refs[j // each][j % each], preferred_element_type=jnp.float32)
            picked = o[:, :head_dim]
            for k in range(1, kv_local):
                picked = jnp.where(
                    row // group == k, o[:, k * head_dim : (k + 1) * head_dim], picked
                )
            acc[owner] = acc[owner] + picked

    @pl.when(step == 2 * blocks - 1)
    def _():
        out_ref[...] = acc[...] / jnp.sum(total[...], axis=-1, keepdims=True)


def attend(queries, new_keys, new_values, k_pool, v_pool, lengths, page_table):
    req_count, kv_local, group, head_dim = queries.shape
    pool_pages, page_size, channels = k_pool.shape
    slots = page_table.shape[1]
    heads = kv_local * group
    per_block = max(b for b in range(1, 17) if pool_pages % b == 0)
    blocks = pool_pages // per_block
    code = page_owners(page_table, lengths, pool_pages, page_size)
    which = jnp.eye(kv_local, dtype=jnp.float32)[None, :, None, :, None]
    spread = (queries.astype(jnp.float32)[:, :, :, None, :] * which).reshape(
        req_count, heads, channels
    )
    pad = ((0, 0), (0, ROWS - heads), (0, 0))
    spread = jnp.pad(spread, pad)

    def by_head(values):
        values = jnp.repeat(values.astype(jnp.float32), group, axis=1)
        return jnp.pad(values, pad)

    streams = max(c for c in range(1, 6) if per_block % c == 0)
    stream_shape = (per_block // streams, page_size, channels)

    def k_spec(t):
        return pl.BlockSpec(
            stream_shape, lambda i, *_: (jnp.minimum(i, blocks - 1) * streams + t, 0, 0)
        )

    def v_spec(t):
        return pl.BlockSpec(
            stream_shape, lambda i, *_: (jnp.maximum(i - blocks, 0) * streams + t, 0, 0)
        )

    whole = pl.BlockSpec((req_count, ROWS, channels), lambda i, *_: (0, 0, 0))
    slim = pl.BlockSpec((req_count, ROWS, head_dim), lambda i, *_: (0, 0, 0))
    out = pl.pallas_call(
        functools.partial(
            attend_kernel, slots, group, blocks, per_block, page_size, head_dim ** (-0.5)
        ),
        out_shape=jax.ShapeDtypeStruct((req_count, ROWS, head_dim), jnp.float32),
        grid_spec=pltpu.PrefetchScalarGridSpec(
            num_scalar_prefetch=2,
            grid=(2 * blocks,),
            in_specs=[
                whole,
                slim,
                slim,
                *[k_spec(t) for t in range(streams)],
                *[v_spec(t) for t in range(streams)],
            ],
            out_specs=slim,
            scratch_shapes=[
                pltpu.VMEM((pool_pages, ROWS, page_size), jnp.float32),
                pltpu.VMEM((req_count, ROWS, page_size), jnp.float32),
                pltpu.VMEM((req_count, ROWS, page_size), jnp.float32),
                pltpu.VMEM((req_count, ROWS, head_dim), jnp.float32),
            ],
        ),
        compiler_params=pltpu.CompilerParams(
            dimension_semantics=("arbitrary",), vmem_limit_bytes=56 * 1024 * 1024
        ),
        cost_estimate=pl.CostEstimate(
            flops=4 * pool_pages * page_size * channels * ROWS,
            bytes_accessed=2 * pool_pages * page_size * channels * 2,
            transcendentals=pool_pages * page_size * ROWS,
        ),
        name="attend_pool",
    )(code, lengths, spread, by_head(new_keys), by_head(new_values), *([k_pool] * streams), *([v_pool] * streams))
    return out[:, :heads]


def pack_kernel(count, send_ref, page_ref, len_ref, *refs):
    outs = refs[2 * MIGP :]
    step = pl.program_id(0)
    page_size = refs[0].shape[1]
    row = lax.broadcasted_iota(jnp.int32, refs[0].shape[1:], 0)
    for s in range(count):

        @pl.when(step == s)
        def _():
            for side in range(2):
                for t in range(MIGP):
                    block = refs[side * MIGP + t][0]
                    keep = row + t * page_size < len_ref[send_ref[s]]
                    outs[s][side, t * page_size : (t + 1) * page_size] = jnp.where(
                        keep, block, jnp.zeros_like(block)
                    )


def pack_blocks(send_rows, page_table, lengths, k_pool, v_pool):
    _, page_size, channels = k_pool.shape
    count = send_rows.shape[0]
    span = MIGP * page_size

    def page_spec(t):
        return pl.BlockSpec(
            (1, page_size, channels),
            lambda i, send_ref, page_ref, len_ref: (page_ref[send_ref[i], t], 0, 0),
        )

    return pl.pallas_call(
        functools.partial(pack_kernel, count),
        out_shape=[jax.ShapeDtypeStruct((2, span, channels), jnp.bfloat16)] * count,
        grid_spec=pltpu.PrefetchScalarGridSpec(
            num_scalar_prefetch=3,
            grid=(count,),
            in_specs=[page_spec(t) for _ in range(2) for t in range(MIGP)],
            out_specs=[pl.BlockSpec((2, span, channels), lambda i, *_: (0, 0, 0))] * count,
        ),
        compiler_params=pltpu.CompilerParams(vmem_limit_bytes=48 * 1024 * 1024),
        name="pack_blocks",
    )(send_rows, page_table, lengths, *([k_pool] * MIGP), *([v_pool] * MIGP))


def place_kernel(count, where_ref, len_ref, fresh_ref, *refs):
    blocks, k_out, v_out = refs[:count], refs[count], refs[count + 1]
    span, channels = blocks[0].shape[1:]
    row = lax.broadcasted_iota(jnp.int32, (span, channels), 0)
    for s in range(count):
        slot = where_ref[s]
        for side, out in enumerate((k_out, v_out)):
            new = fresh_ref[s, :, side * channels : (side + 1) * channels]
            out[slot] = jnp.where(row == len_ref[s], new, blocks[s][side])


def place_blocks(where, lengths, fresh, blocks):
    count = len(blocks)
    _, span, channels = blocks[0].shape
    shape = jax.ShapeDtypeStruct((count, span, channels), jnp.bfloat16)
    smem = pl.BlockSpec(memory_space=pltpu.SMEM)
    vmem = pl.BlockSpec(memory_space=pltpu.VMEM)
    return pl.pallas_call(
        functools.partial(place_kernel, count),
        out_shape=(shape, shape),
        in_specs=[smem, smem, vmem] + [vmem] * count,
        out_specs=(vmem, vmem),
        compiler_params=pltpu.CompilerParams(vmem_limit_bytes=40 * 1024 * 1024),
        name="place_blocks",
    )(where, lengths, fresh, *blocks)


def greet(peers):
    barrier = pltpu.get_barrier_semaphore()
    for peer in peers:
        pl.semaphore_signal(
            barrier, inc=1, device_id=peer, device_id_type=pl.DeviceIdType.MESH
        )
    pl.semaphore_wait(barrier, len(peers))


def send(source, target, send_sem, recv_sem, peer):
    copy = pltpu.make_async_remote_copy(
        src_ref=source,
        dst_ref=target,
        send_sem=send_sem,
        recv_sem=recv_sem,
        device_id=peer,
        device_id_type=pl.DeviceIdType.MESH,
    )
    copy.start()
    return copy


def ring(axis, n):
    me = lax.axis_index(axis)
    return [{axis: lax.rem(me + d, n)} for d in range(1, n)]


def row_norm(pieces, gain_ref, out_ref):
    width = pieces.shape[2]
    n = pieces.shape[0]
    squares = 0.0
    for k in range(n):
        block = pieces[k].astype(jnp.float32)
        squares = squares + jnp.sum(block * block, axis=-1, keepdims=True)
    factor = lax.rsqrt(squares / (n * width) + EPSILON)
    for k in range(n):
        cols = slice(k * width, (k + 1) * width)
        block = pieces[k].astype(jnp.float32)
        out_ref[:, cols] = (block * factor * gain_ref[:, cols]).astype(out_ref.dtype)


def norm_kernel(n, hidden_ref, gain_ref, out_ref, pieces, send_sem, recv_sem):
    me = lax.axis_index("kv")
    peers = ring("kv", n)
    greet(peers)
    copies = [
        send(hidden_ref, pieces.at[me], send_sem.at[d], recv_sem.at[d], peer)
        for d, peer in enumerate(peers)
    ]
    pieces[me] = hidden_ref[...]
    for copy in copies:
        copy.wait()
    row_norm(pieces, gain_ref, out_ref)


def gathered_norm(hidden, gain, n):
    rows, width = hidden.shape
    return pl.pallas_call(
        functools.partial(norm_kernel, n),
        out_shape=jax.ShapeDtypeStruct((rows, n * width), jnp.bfloat16),
        in_specs=[pl.BlockSpec(memory_space=pltpu.VMEM)] * 2,
        out_specs=pl.BlockSpec(memory_space=pltpu.VMEM),
        scratch_shapes=[
            pltpu.VMEM((n, rows, width), jnp.bfloat16),
            pltpu.SemaphoreType.DMA((n - 1,)),
            pltpu.SemaphoreType.DMA((n - 1,)),
        ],
        compiler_params=pltpu.CompilerParams(collective_id=0, has_side_effects=True),
        name="gathered_norm",
    )(hidden, gain[None])


def merge_kernel(
    n, groups, gated_ref, w_ref, hidden_ref, gain_ref, notes_ref,
    mid_ref, normed_ref, got_ref,
    parts, came, mids, got, part_s, part_r, mid_s, mid_r, note_s, note_r,
):
    me = lax.axis_index("kv")
    mine = lax.axis_index("req")
    width = hidden_ref.shape[1]
    peers = ring("kv", n)
    others = ring("req", groups)
    greet(peers + others)
    copies = []
    for d, peer in enumerate(others):
        copies.append(
            send(notes_ref.at[peer["req"]], got.at[mine], note_s.at[d], note_r.at[d], peer)
        )
    got[mine] = notes_ref[mine]

    def part(k):
        cols = pl.ds(pl.multiple_of(k * width, 128), width)
        return jnp.dot(gated_ref[...], w_ref[:, cols], preferred_element_type=jnp.float32)

    part_copies = []
    for d, peer in enumerate(peers):
        parts[d] = part(peer["kv"]).astype(parts.dtype)
        part_copies.append(send(parts.at[d], came.at[d], part_s.at[d], part_r.at[d], peer))
    total = hidden_ref[...].astype(jnp.float32) + part(me)
    for d, copy in enumerate(part_copies):
        copy.wait()
        total = total + came[d].astype(jnp.float32)
    mid_ref[...] = total.astype(mid_ref.dtype)
    mids[me] = total.astype(mid_ref.dtype)
    mid_copies = [
        send(mid_ref, mids.at[me], mid_s.at[d], mid_r.at[d], peer) for d, peer in enumerate(peers)
    ]
    for copy in mid_copies:
        copy.wait()
    row_norm(mids, gain_ref, normed_ref)
    for copy in copies:
        copy.wait()
    got_ref[...] = got[...]


def merged_norm(gated, w_o, hidden, gain, notes, n, groups):
    rows, width = hidden.shape
    dma = pltpu.SemaphoreType.DMA
    vmem = pl.BlockSpec(memory_space=pltpu.VMEM)
    return pl.pallas_call(
        functools.partial(merge_kernel, n, groups),
        out_shape=(
            jax.ShapeDtypeStruct((rows, width), jnp.bfloat16),
            jax.ShapeDtypeStruct((rows, n * width), jnp.bfloat16),
            jax.ShapeDtypeStruct(notes.shape, notes.dtype),
        ),
        in_specs=[vmem] * 5,
        out_specs=(vmem,) * 3,
        scratch_shapes=[
            pltpu.VMEM((n - 1, rows, width), jnp.bfloat16),
            pltpu.VMEM((n - 1, rows, width), jnp.bfloat16),
            pltpu.VMEM((n, rows, width), jnp.bfloat16),
            pltpu.VMEM(notes.shape, notes.dtype),
            dma((n - 1,)), dma((n - 1,)), dma((n - 1,)), dma((n - 1,)),
            dma((groups - 1,)), dma((groups - 1,)),
        ],
        compiler_params=pltpu.CompilerParams(
            collective_id=1, has_side_effects=True, vmem_limit_bytes=32 * 1024 * 1024
        ),
        name="merged_norm",
    )(gated, w_o, hidden, gain[None], notes)


def mlp_kernel(
    n, groups, normed_ref, gate_ref, up_ref, down_ref, mid_ref, out_ref,
    rows, own, pair_out, pair_in, chip_out, chip_in, line_out, line_in,
    a_s, a_r, b_s, b_r, p_s, p_r, c_s, c_r, z_s, z_r,
):
    me = lax.axis_index("req")
    kv = lax.axis_index("kv")
    pairs = groups // 2
    pair, core = me // 2, lax.rem(me, 2)
    sibling = {"req": pair * 2 + 1 - core}
    peers = ring("kv", n)
    far = [{"req": lax.rem(pair + d, pairs) * 2 + core} for d in range(1, pairs)]
    greet(peers + far + [sibling])
    count, width = mid_ref.shape
    across = (((1,), (1,)), ((), ()))

    def at(d):
        return lax.rem(pair - d + pairs, pairs)

    far_copies = [
        send(normed_ref, rows.at[me], a_s.at[d], a_r.at[d], peer) for d, peer in enumerate(far)
    ]
    forwards = [send(normed_ref, rows.at[me], b_s.at[0], b_r.at[0], sibling)]
    rows[me] = normed_ref[...]
    pair_copies = []
    chip_copies = []

    def reduce(d):
        pair_copies[d].wait()
        total = own[d] + pair_in[d].astype(jnp.float32)
        if d == 0:
            own[0] = total
            return
        chip_out[d - 1] = total.astype(chip_out.dtype)
        target = {"req": at(d) * 2 + core}
        chip_copies.append(
            send(chip_out.at[d - 1], chip_in.at[d - 1], c_s.at[d - 1], c_r.at[d - 1], target)
        )

    for d in range(pairs):
        if d > 0:
            far_copies[d - 1].wait()
            held = rows.at[at(d) * 2 + core]
            forwards.append(send(held, held, b_s.at[d], b_r.at[d], sibling))
        forwards[d].wait()
        block = rows[pl.ds(at(d) * 2, 2)].reshape(2 * count, n * width)
        gate = lax.dot_general(block, gate_ref[...], across, preferred_element_type=jnp.float32)
        up = lax.dot_general(block, up_ref[...], across, preferred_element_type=jnp.float32)
        act = (gate / (1.0 + jnp.exp(-gate)) * up).astype(jnp.bfloat16)
        term = jnp.dot(act, down_ref[...], preferred_element_type=jnp.float32)
        low, high = term[:count], term[count:]
        own[d] = jnp.where(core == 0, low, high)
        pair_out[d] = jnp.where(core == 0, high, low).astype(pair_out.dtype)
        pair_copies.append(
            send(pair_out.at[d], pair_in.at[d], p_s.at[d], p_r.at[d], sibling)
        )
        if d > 0:
            reduce(d - 1)
    reduce(pairs - 1)
    for d, copy in enumerate(chip_copies):
        copy.wait()
        own[0] = own[0] + chip_in[d].astype(jnp.float32)
    line_copies = []
    for d, peer in enumerate(peers):
        cols = pl.ds(pl.multiple_of(peer["kv"] * width, 128), width)
        line_out[d] = own[0, :, cols].astype(line_out.dtype)
        line_copies.append(send(line_out.at[d], line_in.at[d], z_s.at[d], z_r.at[d], peer))
    total = mid_ref[...].astype(jnp.float32)
    total = total + own[0, :, pl.ds(pl.multiple_of(kv * width, 128), width)]
    for d, copy in enumerate(line_copies):
        copy.wait()
        total = total + line_in[d].astype(jnp.float32)
    out_ref[...] = total.astype(out_ref.dtype)


def mlp(normed, w_gate, w_up, w_down, mid, n, groups):
    rows, width = mid.shape
    pairs = groups // 2
    wide = n * width
    dma = pltpu.SemaphoreType.DMA
    vmem = pl.BlockSpec(memory_space=pltpu.VMEM)
    half = jnp.bfloat16
    return pl.pallas_call(
        functools.partial(mlp_kernel, n, groups),
        out_shape=jax.ShapeDtypeStruct((rows, width), half),
        in_specs=[vmem] * 5,
        out_specs=vmem,
        scratch_shapes=[
            pltpu.VMEM((groups, rows, wide), half),
            pltpu.VMEM((pairs, rows, wide), jnp.float32),
            pltpu.VMEM((pairs, rows, wide), half),
            pltpu.VMEM((pairs, rows, wide), half),
            pltpu.VMEM((pairs - 1, rows, wide), half),
            pltpu.VMEM((pairs - 1, rows, wide), half),
            pltpu.VMEM((n - 1, rows, width), half),
            pltpu.VMEM((n - 1, rows, width), half),
            dma((pairs - 1,)), dma((pairs - 1,)),
            dma((pairs,)), dma((pairs,)),
            dma((pairs,)), dma((pairs,)),
            dma((pairs - 1,)), dma((pairs - 1,)),
            dma((n - 1,)), dma((n - 1,)),
        ],
        compiler_params=pltpu.CompilerParams(
            collective_id=2, has_side_effects=True, vmem_limit_bytes=48 * 1024 * 1024
        ),
        name="mlp_exchange",
    )(normed, w_gate.T, w_up.T, w_down.T, mid)


def per_device(
    hidden,
    attn_gain,
    q_gain,
    k_gain,
    w_q,
    w_gate_attn,
    w_k,
    w_v,
    w_o,
    k_pool,
    v_pool,
    lengths,
    page_table,
    mig_request,
    mig_dest,
    mlp_gain,
    w_gate,
    w_up,
    w_down,
):
    head_dim = q_gain.shape[0]
    req_count = hidden.shape[0]
    kv_local = w_k.shape[1] // head_dim
    q_local = w_q.shape[1] // head_dim
    group_size = q_local // kv_local
    channels = kv_local * head_dim
    req_groups = lax.axis_size("req")
    me = lax.axis_index("req")

    mig_rows = mig_request[0]
    dest_row = mig_dest[0]
    partner = me ^ jnp.arange(req_groups, dtype=jnp.int32)
    chosen = dest_row[None, :] == partner[:, None]
    send_rows = jnp.sum(jnp.where(chosen, mig_rows[None, :], 0), axis=1)
    kv_count = lax.axis_size("kv")
    packed = pack_blocks(send_rows, page_table, lengths, k_pool, v_pool)
    packed, hidden = lax.optimization_barrier((packed, hidden))
    arrived = [packed[0]] + [
        lax.ppermute(packed[s], "req", [(i, i ^ s) for i in range(req_groups)])
        for s in range(1, req_groups)
    ]

    normed = gathered_norm(hidden, attn_gain, kv_count)
    normed, arrived[1] = lax.optimization_barrier((normed, arrived[1]))
    query_raw = jnp.dot(normed, w_q, preferred_element_type=jnp.float32).reshape(
        req_count, q_local, head_dim
    )
    gate_raw = jnp.dot(normed, w_gate_attn, preferred_element_type=jnp.float32)
    key_raw = jnp.dot(normed, w_k, preferred_element_type=jnp.float32).reshape(
        req_count, kv_local, head_dim
    )
    value_raw = jnp.dot(normed, w_v, preferred_element_type=jnp.float32).reshape(
        req_count, kv_local, head_dim
    )
    queries = rotate(rms_norm(query_raw, q_gain), lengths).astype(jnp.bfloat16)
    queries = queries.reshape(req_count, kv_local, group_size, head_dim)
    new_keys = rotate(rms_norm(key_raw, k_gain), lengths).astype(jnp.bfloat16)
    new_values = value_raw.astype(jnp.bfloat16)

    fresh = jnp.concatenate(
        [new_keys.reshape(req_count, channels), new_values.reshape(req_count, channels)], axis=1
    )
    by_dest = jnp.sum(
        jnp.where(
            dest_row[None, :] == jnp.arange(req_groups, dtype=jnp.int32)[:, None],
            mig_rows[None, :],
            0,
        ),
        axis=1,
    )
    dest_len = lengths[by_dest].astype(jnp.float32)
    width = 2 * channels
    notes = jnp.concatenate(
        [fresh[by_dest].astype(jnp.float32), jnp.broadcast_to(dest_len[:, None], (req_groups, 128))],
        axis=1,
    )
    notes = jnp.broadcast_to(notes[:, None, :], (req_groups, 8, width + 128))
    context = attend(queries, new_keys, new_values, k_pool, v_pool, lengths, page_table)
    context, arrived[2] = lax.optimization_barrier((context, arrived[2]))
    gated = (jax.nn.sigmoid(gate_raw) * context.reshape(req_count, q_local * head_dim)).astype(
        jnp.bfloat16
    )
    mid_slice, normed_mlp, got = merged_norm(
        gated, w_o, hidden, mlp_gain, notes, kv_count, req_groups
    )
    arrived, normed_mlp = lax.optimization_barrier((arrived, normed_mlp))
    mine = got[partner, 0]
    got_len = mine[:, width].astype(jnp.int32)
    mig_keys, mig_values = place_blocks(
        partner, got_len, mine[:, None, :width].astype(jnp.bfloat16), arrived
    )
    out_hidden = mlp(normed_mlp, w_gate, w_up, w_down, mid_slice, kv_count, req_groups)
    return (out_hidden, mig_keys, mig_values)


def solution(mesh):
    return jax.shard_map(
        per_device,
        mesh=mesh,
        in_specs=(
            P("req", "kv"),
            P(),
            P(),
            P(),
            P(None, "kv"),
            P(None, "kv"),
            P(None, "kv"),
            P(None, "kv"),
            P("kv", None),
            P("req", None, "kv"),
            P("req", None, "kv"),
            P("req"),
            P("req", None),
            P("req", None),
            P("req", None),
            P(),
            P(None, ("req", "kv")),
            P(None, ("req", "kv")),
            P(None, ("req", "kv")),
        ),
        out_specs=(P("req", "kv"), P("req", None, "kv"), P("req", None, "kv")),
        check_vma=False,
    )
```
